32 devices in a mesh: layer: 4 (over z), feat: 8 (over y, x, core).
Axes of the slice: x: 2, y: 2, z: 4, core: 2. Of those that a mesh axis runs over, the one named last changes fastest.
Arguments:
- residuals: bfloat16 [4, 64, 4608], P('layer', 'feat'), may hold values from -60 to 60
- enc_weight: bfloat16 [4, 4608, 16384], P('layer', None, 'feat'), may hold values from -0.09375 to 0.09375
- enc_bias: float32 [4, 16384], P('layer', 'feat'), may hold values from -3 to 3
- thresh_levels: int32 [4, 16384], P('layer', 'feat'), may hold values from 2 to 8
- dec_weight: bfloat16 [4, 4, 4608, 16384], P('layer', None, 'feat'), may hold values from -0.046875 to 0.046875
- dec_bias: float32 [4, 4608], P('layer', 'feat'), may hold values from -3 to 3
Outputs:
- recon: bfloat16 [4, 64, 4608], P('layer', None, 'feat')
The draws below stay inside these ranges and needn't reach their ends.
All inputs are finite; a program needn't handle non-finite values.
Results may differ from the reference program's by a relative error of at most 0.0053.
Values may be sent and summed in bfloat16 or wider, within the bound.
A program may use at most 192 MiB of HBM per device.

```python
import math
import jax
import jax.numpy as jnp
from jax import lax

D = 4608
FEATURES = 16384
LAYERS = 4
TOKENS = 64


def draw_residuals(key, part):
    first_key, second_key = jax.random.split(jax.random.fold_in(key, 11))
    base = jnp.clip(jax.random.normal(first_key, (LAYERS, TOKENS, D), jnp.float32), -6.0, 6.0)
    scales = jnp.exp(jax.random.uniform(second_key, (LAYERS, TOKENS, 1), jnp.float32, 0.0, math.log(10.0)))
    return (base * scales).astype(jnp.bfloat16)


def dense_groups(key):
    block_size = 64
    groups = FEATURES // block_size
    chosen = max(1, groups // 4)
    layer_keys = jax.random.split(jax.random.fold_in(key, 23), LAYERS)

    def order_one(layer_key):
        return jax.random.permutation(layer_key, groups)
    orders = jax.vmap(order_one)(layer_keys)
    marks = orders < chosen
    return jnp.repeat(marks, block_size, axis=1)


def draw_thresh_levels(key, part):
    dense = dense_groups(key)
    levels = jax.random.randint(jax.random.fold_in(key, 31), (LAYERS, FEATURES), 2, 9)
    return jnp.where(dense, 2, levels).astype(jnp.int32)


def draw_enc_bias(key, part):
    dense = dense_groups(key)
    first_key, second_key = jax.random.split(jax.random.fold_in(key, 37))
    spread = jnp.clip(0.5 * jax.random.normal(first_key, (LAYERS, FEATURES), jnp.float32), -3.0, 3.0)
    high = jax.random.uniform(second_key, (LAYERS, FEATURES), jnp.float32, 2.0, 3.0)
    return jnp.where(dense, high, spread).astype(jnp.float32)


def steps_of(own_key, shape, cuts, least, top_value):
    def one(axis_at, parts):
        steps = jax.random.uniform(jax.random.fold_in(jax.random.fold_in(own_key, 6), axis_at), (parts,), jnp.float32, least / len(cuts), top_value / len(cuts))
        return jnp.repeat(jnp.exp(steps), shape[axis_at] // parts).reshape((-1,) + (1,) * (len(shape) - axis_at - 1))

    level = one(*cuts[0])
    for cut in cuts[1:]:
        level = level * one(*cut)
    return level


def centred(own_key, shape, deviation, limit, pieces=(), dtype=jnp.bfloat16):
    values = jax.random.normal(own_key, shape, jnp.float32) * deviation
    if len(pieces) > 0:
        values = steps_of(own_key, shape, pieces, -0.22, 0.18) * values
    return jnp.clip(values, min=-limit, max=limit).astype(dtype)


def setup_inputs(seed: int = 0) -> dict:
    keys = jax.random.split(jax.random.key(seed), 7)
    return {
        "residuals": draw_residuals(jax.random.fold_in(keys[6], 71), 0),
        "enc_weight": centred(keys[1], (LAYERS, D, FEATURES), D ** -0.5, 0.09375, ((0, 4), (2, 8))),
        "enc_bias": draw_enc_bias(jax.random.fold_in(keys[6], 71), 0),
        "thresh_levels": draw_thresh_levels(jax.random.fold_in(keys[6], 71), 0),
        "dec_weight": centred(keys[4], (LAYERS, LAYERS, D, FEATURES), FEATURES ** -0.5, 0.046875, ((0, 4), (2, 8))),
        "dec_bias": centred(keys[5], (LAYERS, D), 0.5, 3.0, ((0, 4), (1, 8)), jnp.float32),
    }


def encode(resid, enc_matrix, bias_row, levels):
    resid_float = resid.astype(jnp.float32)
    factor = lax.rsqrt(lax.optimization_barrier(jnp.mean(resid_float * resid_float, axis=-1, keepdims=True)) + 1e-06)
    normed = (resid_float * factor).astype(jnp.bfloat16)
    pre = jnp.dot(normed, enc_matrix, preferred_element_type=jnp.float32) + bias_row
    theta = levels.astype(jnp.float32) * 0.125
    return (pre * jnp.clip((pre - theta) / 0.25, 0.0, 1.0)).astype(jnp.bfloat16)

def reference(residuals, enc_weight, enc_bias, thresh_levels, dec_weight, dec_bias):
    activations = [encode(residuals[i], enc_weight[i], enc_bias[i], thresh_levels[i]) for i in range(LAYERS)]
    results = []
    for target in range(LAYERS):
        total = jnp.zeros((TOKENS, D), jnp.float32)
        for source in range(target + 1):
            total = total + jnp.dot(activations[source], dec_weight[source, target].T, preferred_element_type=jnp.float32)
        results.append((total + dec_bias[target]).astype(jnp.bfloat16))
    return jnp.stack(results)
```

```python
import functools

import jax
import jax.numpy as jnp
from jax import lax
from jax.experimental import pallas as pl
from jax.experimental.pallas import tpu as pltpu
from jax.sharding import PartitionSpec as P

MESH = pl.DeviceIdType.MESH
VMEM_BYTES = 63 * 2**20
VMEM_SPARE = 3 * 2**20


def plain(residuals, enc_weight, enc_bias, thresh_levels, dec_weight, dec_bias):
    layers = dec_weight.shape[1]
    my_layer = lax.axis_index("layer")
    theta = thresh_levels[0].astype(jnp.float32) * 0.125
    keep = (jnp.arange(layers) >= my_layer)[:, None, None]
    resid_float = lax.all_gather(residuals, "feat", axis=1, tiled=True)[0].astype(jnp.float32)
    factor = lax.rsqrt(jnp.mean(resid_float * resid_float, axis=-1, keepdims=True) + 1e-06)
    normed = (resid_float * factor).astype(jnp.bfloat16)
    pre = jnp.dot(normed, enc_weight[0], preferred_element_type=jnp.float32) + enc_bias[0]
    activity = (pre * jnp.clip((pre - theta) / 0.25, 0.0, 1.0)).astype(jnp.bfloat16)
    partials = jnp.einsum(
        "rf,edf->erd",
        lax.all_gather(activity, "feat", axis=1, tiled=True),
        dec_weight[0],
        preferred_element_type=jnp.float32,
    )
    partials = jnp.where(keep, partials, 0.0)
    total = lax.psum_scatter(partials, "layer", scatter_dimension=0, tiled=True)
    return (total + dec_bias[0]).astype(jnp.bfloat16)


def xor(a, b, size):
    out, bit = 0, 1
    while bit < size:
        x, y = lax.rem(lax.div(a, bit), 2), lax.rem(lax.div(b, bit), 2)
        out = out + bit * (x + y - 2 * x * y)
        bit *= 2
    return out


def kernel(
    layers, n, parts, slots,
    resid_ref, enc_ref, bias_ref, level_ref, dec_ref, dbias_ref, out_ref,
    gathered, normed, enc_buf, acts, dec_buf, acc, outbox, inbox,
    res_send, res_recv, resf_send, resf_recv,
    act_send, act_recv, actf_send, actf_recv,
    sum_send, sum_recv, enc_sem, dec_sem,
):
    chips = n // 2
    layer = lax.axis_index("layer")
    feat = lax.axis_index("feat")
    chip, core = lax.div(feat, 2), lax.rem(feat, 2)
    mate = feat + 1 - 2 * core
    rows = resid_ref.shape[1]
    width = resid_ref.shape[2]
    half = width // 2
    cols = acts.shape[3]
    dests = layers - layer
    total = dests * n
    near = n // 2

    def block_of(place):
        other = xor(chip, lax.div(place, 2), chips)
        side = lax.rem(place, 2)
        return 2 * other + core + side - 2 * core * side

    def partner(k):
        return mate if k == 0 else 2 * xor(chip, jnp.int32(k), chips) + core

    def step_of(c):
        early = c < near * dests
        late = c - near * dests
        place = jnp.where(early, lax.div(c, dests), near + lax.rem(late, n - near))
        dest = jnp.where(early, lax.rem(c, dests), lax.div(late, n - near))
        return place, layers - 1 - dest

    def dec_copy(c):
        place, dest = step_of(c)
        size = parts * cols
        start = pl.multiple_of(block_of(place) * size, size)
        slot = lax.rem(c, slots)
        return pltpu.make_async_copy(
            dec_ref.at[0, dest, :, pl.ds(start, size)], dec_buf.at[slot], dec_sem.at[slot]
        )

    def enc_copy(i):
        return pltpu.make_async_copy(
            enc_ref.at[0, :, pl.ds(pl.multiple_of(i * cols, cols), cols)],
            enc_buf.at[i], enc_sem.at[i],
        )

    def remote(src, dst, send, recv, where):
        return pltpu.make_async_remote_copy(
            src_ref=src, dst_ref=dst, send_sem=send, recv_sem=recv,
            device_id=where, device_id_type=MESH,
        )

    def res_copy(k):
        return remote(gathered.at[feat], gathered.at[feat], res_send.at[k], res_recv.at[k],
                      (layer, partner(k)))

    def resf_copy(k):
        block = partner(k)
        return remote(gathered.at[block], gathered.at[block], resf_send.at[k], resf_recv.at[k],
                      (layer, mate))

    def act_copy(k, i):
        return remote(acts.at[feat, i], acts.at[feat, i], act_send.at[k, i], act_recv.at[k, i],
                      (layer, partner(k)))

    def actf_copy(k):
        block = 2 * xor(chip, k, chips) + core
        return remote(acts.at[block], acts.at[block], actf_send.at[k], actf_recv.at[k],
                      (layer, mate))

    def sum_copy(dest):
        return remote(outbox.at[dest], inbox.at[layer], sum_send.at[dest], sum_recv.at[layer],
                      (dest, feat))

    for i in range(parts):
        enc_copy(i).start()

    barrier = pltpu.get_barrier_semaphore()
    for k in range(chips):
        pl.semaphore_signal(barrier, inc=1, device_id=(layer, partner(k)), device_id_type=MESH)
    for k in range(1, layers):
        pl.semaphore_signal(barrier, inc=1, device_id=(lax.rem(layer + k, layers), feat),
                            device_id_type=MESH)

    x = resid_ref[0].astype(jnp.float32)
    x = x * lax.rsqrt(jnp.mean(x * x, axis=-1, keepdims=True) + 1e-06)
    gathered[feat] = jnp.concatenate([x[:, :half], x[:, half:]], axis=0).astype(jnp.bfloat16)

    pl.semaphore_wait(barrier, chips + layers - 1)
    for k in range(chips - 1, -1, -1):
        res_copy(k).start()
    first = min(2, slots)

    def prefetch(c, carry):
        @pl.when(c < total)
        def _():
            dec_copy(c).start()
        return carry

    lax.fori_loop(0, first, prefetch, 0)
    acc[...] = jnp.zeros_like(acc)
    for k in range(1, chips):
        res_copy(k).wait_recv()
        resf_copy(k).start()
    res_copy(0).wait_recv()
    for k in range(1, chips):
        resf_copy(k).wait_recv()

    for pair in range(n // 2):
        low = gathered[2 * pair].astype(jnp.float32)
        high = gathered[2 * pair + 1].astype(jnp.float32)
        at = pl.ds(2 * rows * pair, 2 * rows)
        normed[at, :half] = jnp.concatenate([low[:rows], high[:rows]], axis=0).astype(jnp.bfloat16)
        normed[at, half:] = jnp.concatenate([low[rows:], high[rows:]], axis=0).astype(jnp.bfloat16)

    each = -(-(slots - first) // parts)

    def encode(i, carry):
        enc_copy(i).wait()
        lax.fori_loop(first + i * each, jnp.minimum(first + (i + 1) * each, slots), prefetch, 0)
        here = pl.ds(pl.multiple_of(i * cols, cols), cols)
        pre = jnp.dot(normed[...], enc_buf[i], preferred_element_type=jnp.float32)
        pre = pre + bias_ref[:, here]
        theta = level_ref[:, here].astype(jnp.float32) * 0.125
        acts[feat, i] = (pre * jnp.clip((pre - theta) * 4.0, 0.0, 1.0)).astype(jnp.bfloat16)
        for k in range(chips):
            act_copy(k, i).start()
        return carry

    lax.fori_loop(0, parts, encode, 0)

    def arrive(place):
        k = lax.div(place, 2)
        direct = jnp.logical_or(place == 1, jnp.logical_and(place > 1, lax.rem(place, 2) == 0))

        @pl.when(direct)
        def _():
            for i in range(parts):
                remote(acts.at[feat, i], acts.at[feat, i], act_send.at[k, i], act_recv.at[k, i],
                       (layer, mate)).wait_recv()

        @pl.when(jnp.logical_and(direct, place > 1))
        def _():
            actf_copy(k).start()

        @pl.when(jnp.logical_and(place > 1, lax.rem(place, 2) == 1))
        def _():
            actf_copy(k).wait_recv()

    def decode(c, carry):
        place, dest = step_of(c)

        @pl.when(dest == layers - 1)
        def _():
            arrive(place)

        block = block_of(place)
        slot = lax.rem(c, slots)
        dec_copy(c).wait()
        part = acc[dest]
        for i in range(parts):
            part = part + lax.dot_general(
                dec_buf[slot, :, i * cols:(i + 1) * cols], acts[block, i],
                (((1,), (1,)), ((), ())), preferred_element_type=jnp.float32,
            )
        acc[dest] = part

        @pl.when(c + slots < total)
        def _():
            dec_copy(c + slots).start()

        @pl.when(jnp.logical_and(place == n - 1, dest > layer))
        def _():
            outbox[dest] = acc[dest].T
            sum_copy(dest).start()

        return carry

    lax.fori_loop(0, total, decode, 0)

    result = acc[layer].T + dbias_ref[...]
    outbox[layer] = result
    for source in range(layers - 1):
        @pl.when(source < layer)
        def _():
            remote(outbox.at[0], inbox.at[source], sum_send.at[0], sum_recv.at[source],
                   (layer, mate)).wait_recv()
            outbox[layer] = outbox[layer] + inbox[source]
    out_ref[0] = outbox[layer].astype(jnp.bfloat16)

    for k in range(chips):
        res_copy(k).wait_send()
        for i in range(parts):
            act_copy(k, i).wait_send()
    for k in range(1, chips):
        resf_copy(k).wait_send()
        actf_copy(jnp.int32(k)).wait_send()
    for dest in range(1, layers):
        @pl.when(dest > layer)
        def _():
            sum_copy(dest).wait_send()


def fused(layers, n, residuals, enc_weight, enc_bias, thresh_levels, dec_weight, dec_bias):
    rows, width = residuals.shape[1:]
    features = enc_weight.shape[2]
    out_rows = dec_weight.shape[2]
    tokens = rows * n
    chips = n // 2
    parts = 4
    cols = features // parts
    pad = lambda x: -(-x // 128) * 128
    fixed = (
        2 * n * rows * width * 2 + width * features * 2 + n * tokens * features * 2
        + layers * out_rows * pad(tokens) * 4 + 2 * layers * tokens * pad(out_rows) * 4
        + rows * width * 2 + 4 * 8 * features * 4 + tokens * pad(out_rows) * 2
    )
    slot_bytes = out_rows * features * 2
    slots = max(1, min(layers * n, (VMEM_BYTES - VMEM_SPARE - fixed) // slot_bytes))
    dma = pltpu.SemaphoreType.DMA
    vmem = pl.BlockSpec(memory_space=pltpu.VMEM)
    hbm = pl.BlockSpec(memory_space=pl.ANY)
    weights = width * features + layers * out_rows * features * n
    return pl.pallas_call(
        functools.partial(kernel, layers, n, parts, slots),
        out_shape=jax.ShapeDtypeStruct((1, tokens, out_rows), jnp.bfloat16),
        in_specs=[vmem, hbm, vmem, vmem, hbm, vmem],
        out_specs=vmem,
        scratch_shapes=[
            pltpu.VMEM((n, 2 * rows, width // 2), jnp.bfloat16),
            pltpu.VMEM((tokens, width), jnp.bfloat16),
            pltpu.VMEM((parts, width, cols), jnp.bfloat16),
            pltpu.VMEM((n, parts, tokens, cols), jnp.bfloat16),
            pltpu.VMEM((slots, out_rows, features), jnp.bfloat16),
            pltpu.VMEM((layers, out_rows, tokens), jnp.float32),
            pltpu.VMEM((layers, tokens, out_rows), jnp.float32),
            pltpu.VMEM((layers, tokens, out_rows), jnp.float32),
            dma((chips,)), dma((chips,)), dma((chips,)), dma((chips,)),
            dma((chips, parts)), dma((chips, parts)), dma((chips,)), dma((chips,)),
            dma((layers,)), dma((layers,)), dma((parts,)), dma((slots,)),
        ],
        compiler_params=pltpu.CompilerParams(
            collective_id=0, has_side_effects=True, vmem_limit_bytes=VMEM_BYTES
        ),
        cost_estimate=pl.CostEstimate(
            flops=2 * tokens * weights, bytes_accessed=2 * weights, transcendentals=0
        ),
    )(residuals, enc_weight, enc_bias, thresh_levels, dec_weight, dec_bias)


def solution(mesh):
    layers, n = mesh.shape["layer"], mesh.shape["feat"]

    def per_device(*args):
        residuals, enc_weight, _, _, dec_weight, _ = args
        fits = (
            dec_weight.shape[1] == layers
            and n >= 4 and n & (n - 1) == 0
            and residuals.shape[1] % 8 == 0
            and residuals.shape[2] % 256 == 0
            and enc_weight.shape[2] % 1024 == 0
            and dec_weight.shape[2] % 16 == 0
        )
        return fused(layers, n, *args) if fits else plain(*args)

    in_specs = (
        P("layer", "feat", None),
        P("layer", None, "feat"),
        P("layer", "feat"),
        P("layer", "feat"),
        P("layer", None, "feat", None),
        P("layer", "feat"),
    )
    out_specs = P("layer", None, "feat")
    return jax.shard_map(
        per_device, mesh=mesh, in_specs=in_specs, out_specs=out_specs, check_vma=False
    )
```
